256 devices in a mesh: dp: 16 (over z, x_lo), token: 16 (over y, x_hi, core).
Axes of the slice: x: 4 (x_hi: 2, x_lo: 2; x = x_hi * 2 + x_lo), y: 4, z: 8, core: 2. Of those that a mesh axis runs over, the one named last changes fastest.
Arguments:
- tokens: bfloat16 [1024, 16, 1536], P('dp', 'token'), may hold values from -180 to 180
- grad_out: bfloat16 [1024, 16, 1536], P('dp', 'token'), may hold values from -36 to 36
- gain: float32 [16, 1536], P('token'), may hold values from 0.1 to 1.9
- w_gate: bfloat16 [16, 1536, 6144], P('token', None, 'dp'), may hold values from -0.15625 to 0.15625
- w_up: bfloat16 [16, 1536, 6144], P('token', None, 'dp'), may hold values from -0.15625 to 0.15625
- w_down: bfloat16 [16, 6144, 1536], P('token', 'dp'), may hold values from -0.078125 to 0.078125
Outputs:
- d_tokens: bfloat16 [1024, 16, 1536], P('dp', 'token')
- d_w_gate: bfloat16 [16, 1536, 6144], P('token', None, 'dp')
- d_w_up: bfloat16 [16, 1536, 6144], P('token', None, 'dp')
- d_w_down: bfloat16 [16, 6144, 1536], P('token', 'dp')
- d_gain: float32 [16, 1536], P('token')
The draws below stay inside these ranges and needn't reach their ends.
All inputs are finite; a program needn't handle non-finite values.
Results may differ from the reference program's by a relative error of at most 0.023.
Values may be sent and summed in bfloat16 or wider, within the bound.
No kernel may reach another device: no remote copies, remote signals or barrier semaphores. Data moves between devices by JAX's collectives and lax.ppermute only.
A program may use at most 128 MiB of HBM per device.

```python
import math
import jax
import jax.numpy as jnp
from jax import lax

D = 1536
FF = 6144
TOKENS = 16
SAMPLES = 1024


def draw_tokens(key, part):
    key = jax.random.fold_in(key, 11)
    key_rows, key_cols, key_base = jax.random.split(key, 3)
    row_scale = jnp.exp(jax.random.uniform(key_rows, (SAMPLES, TOKENS, 1), jnp.float32, 0.0, math.log(10.0)))
    col_scale = jnp.exp(jax.random.uniform(key_cols, (1, 1, D), jnp.float32, math.log(0.3), math.log(3.0)))
    base = jnp.clip(jax.random.normal(key_base, (SAMPLES, TOKENS, D), jnp.float32), -6.0, 6.0)
    return (base * row_scale * col_scale).astype(jnp.bfloat16)


def draw_grad_out(key, part):
    key = jax.random.fold_in(key, 12)
    key_rows, key_base = jax.random.split(key, 2)
    row_scale = jnp.exp(jax.random.uniform(key_rows, (SAMPLES, TOKENS, 1), jnp.float32, math.log(0.5), math.log(2.0)))
    rising = 1.0 + 2.0 * jnp.arange(SAMPLES, dtype=jnp.float32).reshape(SAMPLES, 1, 1) / SAMPLES
    base = jnp.clip(jax.random.normal(key_base, (SAMPLES, TOKENS, D), jnp.float32), -6.0, 6.0)
    return (base * row_scale * rising).astype(jnp.bfloat16)


def level_of(own_key, shape, cuts, low, largest):
    factor_of, own = 1.0, jax.random.fold_in(own_key, 6)
    for axis_at, shards_of in cuts:
        steps = jnp.exp(jax.random.uniform(jax.random.fold_in(own, axis_at), (shards_of,), jnp.float32, low / len(cuts), largest / len(cuts)))
        factor_of = factor_of * jnp.repeat(steps, shape[axis_at] // shards_of).reshape([-1 if axis == axis_at else 1 for axis in range(len(shape))])
    return factor_of


def bell_draw(own_key, extent, spread, reach, pieces=(), held_as=jnp.bfloat16):
    loudness = level_of(own_key, extent, pieces, -0.22, 0.18) if pieces else 1.0
    values = jax.random.normal(own_key, extent, jnp.float32) * spread * loudness
    return jnp.minimum(jnp.maximum(values, -reach), reach).astype(held_as)


def setup_inputs(seed: int = 0) -> dict:
    seeds = jax.random.split(jax.random.key(seed), 7)
    tokens = draw_tokens(jax.random.fold_in(seeds[6], 71), 0)
    grad_out = draw_grad_out(jax.random.fold_in(seeds[6], 71), 0)
    gain = jnp.clip(1.0 + 0.18 * jax.random.normal(seeds[2], (TOKENS, D), jnp.float32), 0.1, 1.9)
    w_gate = bell_draw(seeds[3], (TOKENS, D, FF), D ** -0.5, 0.15625, ((0, 16), (2, 16)))
    w_up = bell_draw(seeds[4], (TOKENS, D, FF), D ** -0.5, 0.15625, ((0, 16), (2, 16)))
    w_down = bell_draw(seeds[5], (TOKENS, FF, D), FF ** -0.5, 0.078125, ((0, 16), (1, 16)))
    return {"tokens": tokens, "grad_out": grad_out, "gain": gain, "w_gate": w_gate, "w_up": w_up, "w_down": w_down}


def mix_heads(source):
    shape = source.shape
    split = source.reshape(shape[0], TOKENS, TOKENS, D // TOKENS)
    return jnp.swapaxes(split, 1, 2).reshape(shape)

def token_backward(inputs):
    hid_rows, grad_rows, gate_mat, up_mat, down_mat = inputs
    gate_out = jnp.dot(hid_rows, gate_mat, preferred_element_type=jnp.float32)
    up_out = jnp.dot(hid_rows, up_mat, preferred_element_type=jnp.float32)
    sigmoid_gate = jax.nn.sigmoid(gate_out)
    silu_gate = gate_out * sigmoid_gate
    activation = (silu_gate * up_out).astype(jnp.bfloat16)
    d_activation = jnp.dot(grad_rows, down_mat.T, preferred_element_type=jnp.float32)
    d_down = jnp.dot(activation.T, grad_rows, preferred_element_type=jnp.float32).astype(jnp.bfloat16)
    silu_slope = sigmoid_gate * (1.0 + gate_out * (1.0 - sigmoid_gate))
    d_gate_pre = (d_activation * up_out * silu_slope).astype(jnp.bfloat16)
    d_up_pre = (d_activation * silu_gate).astype(jnp.bfloat16)
    d_gate = jnp.dot(hid_rows.T, d_gate_pre, preferred_element_type=jnp.float32).astype(jnp.bfloat16)
    d_up = jnp.dot(hid_rows.T, d_up_pre, preferred_element_type=jnp.float32).astype(jnp.bfloat16)
    d_hidden = jnp.dot(d_gate_pre, gate_mat.T, preferred_element_type=jnp.float32) + jnp.dot(d_up_pre, up_mat.T, preferred_element_type=jnp.float32)
    return (d_hidden, d_gate, d_up, d_down)

def reference(tokens, grad_out, gain, w_gate, w_up, w_down):
    summed = tokens.astype(jnp.float32) + mix_heads(tokens).astype(jnp.float32)
    mean_square = lax.optimization_barrier(jnp.mean(summed * summed, axis=-1, keepdims=True))
    inv_rms = lax.rsqrt(mean_square + 1e-06)
    normed = summed * inv_rms
    hidden_in = (normed * gain[None]).astype(jnp.bfloat16)
    d_hidden, d_w_gate, d_w_up, d_w_down = lax.map(token_backward, (jnp.swapaxes(hidden_in, 0, 1), jnp.swapaxes(grad_out, 0, 1), w_gate, w_up, w_down))
    d_hidden = jnp.swapaxes(d_hidden, 0, 1)
    d_gain = lax.optimization_barrier(jnp.sum(d_hidden * normed, axis=0))
    scaled = d_hidden * gain[None]
    d_summed = grad_out.astype(jnp.float32) + inv_rms * (scaled - normed * lax.optimization_barrier(jnp.mean(scaled * normed, axis=-1, keepdims=True)))
    d_tokens = (d_summed + mix_heads(d_summed)).astype(jnp.bfloat16)
    return (d_tokens, d_w_gate, d_w_up, d_w_down, d_gain)
```

```python
import jax
import jax.numpy as jnp
from jax import lax
from jax.sharding import PartitionSpec as P

BF = jnp.bfloat16
F32 = jnp.float32


def cat(*parts):
    return jnp.concatenate(parts, axis=0)


def moves(size):
    ring = size // 2

    def at(z, x):
        return (z % ring) * 2 + x

    places = [(z, x) for z in range(ring) for x in range(2)]
    down = [(at(z, x), at(z - 1, x)) for z, x in places]
    rise = [(at(z, x), at(z + 1, x)) for z, x in places]
    swap = [(at(z, x), at(z, 1 - x)) for z, x in places]

    def from_above(block):
        return lax.ppermute(block, "dp", down)

    def from_below(block):
        return lax.ppermute(block, "dp", rise)

    def from_pair(block):
        return lax.ppermute(block, "dp", swap)

    return from_above, from_below, from_pair


def gather(own, hops):
    above, below, pair = hops
    rows = own.shape[0]
    half = rows // 2
    up1, dn1, pair0 = above(own), below(own), pair(own)
    first = [own, up1, dn1, pair0]

    up = above(cat(up1, pair0[:half]))
    dn = below(cat(dn1, pair0[:half]))
    side = pair(cat(up1[half:], dn1[half:]))
    second = [up, dn, side]

    up_b = above(up)
    dn_b = below(dn)
    side_b = pair(cat(up[half:rows], dn[half:rows]))
    third = [up_b, dn_b, side_b]

    up_c = above(cat(up_b[:half], up_b[rows:]))
    dn_c = below(cat(dn_b[half:rows], dn_b[rows:]))
    side_c = pair(cat(up_b[half:rows], dn_b[half:rows]))
    fourth = [up_c, dn_c, side_c]

    last = [pair(cat(up_c[:half], dn_c[:half]))]
    return [cat(*group) for group in (first, second, third, fourth)] + [last[0]]


def scatter_sum(parts, rows, hops):
    above, below, pair = hops
    half = rows // 2

    def add(part, *arrived):
        total = part
        for one in arrived:
            total = total + one.astype(F32)
        return total

    def sent(block):
        return block.astype(BF)

    first, second, third, fourth, last = parts
    own, up1, dn1, pair0 = (first[i * rows : (i + 1) * rows] for i in range(4))
    wide = rows + half
    up2, dn2, side1 = second[:wide], second[wide : 2 * wide], second[2 * wide :]
    up3, dn3, side2 = third[:wide], third[wide : 2 * wide], third[2 * wide :]
    up4, dn4, side3 = fourth[:rows], fourth[rows : 2 * rows], fourth[2 * rows :]

    got = pair(sent(last))
    up4 = sent(cat(add(up4[:half], got[:half]), up4[half:]))
    dn4 = sent(cat(add(dn4[:half], got[half:]), dn4[half:]))

    from_dn, from_up, got = below(up4), above(dn4), pair(sent(side3))
    up3 = sent(cat(add(up3[:half], from_dn[:half]), add(up3[half:rows], got[:half]), add(up3[rows:], from_dn[half:])))
    dn3 = sent(cat(dn3[:half], add(dn3[half:rows], from_up[:half], got[half:]), add(dn3[rows:], from_up[half:])))

    from_dn, from_up, got = below(up3), above(dn3), pair(sent(side2))
    up2 = sent(cat(add(up2[:half], from_dn[:half]), add(up2[half:rows], from_dn[half:rows], got[:half]), add(up2[rows:], from_dn[rows:])))
    dn2 = sent(cat(add(dn2[:half], from_up[:half]), add(dn2[half:rows], from_up[half:rows], got[half:]), add(dn2[rows:], from_up[rows:])))

    from_dn, from_up, got = below(up2), above(dn2), pair(sent(side1))
    up1 = sent(cat(add(up1[:half], from_dn[:half]), add(up1[half:], from_dn[half:rows], got[:half])))
    dn1 = sent(cat(add(dn1[:half], from_up[:half]), add(dn1[half:], from_up[half:rows], got[half:])))
    pair0 = sent(cat(add(pair0[:half], from_dn[rows:], from_up[rows:]), pair0[half:]))

    from_dn, from_up, got = below(up1), above(dn1), pair(pair0)
    return add(own, from_dn, from_up, got)


def dot(a, b, dims):
    return lax.dot_general(a, b, ((dims[0], dims[1]), ((), ())), preferred_element_type=F32)


def shards(tokens, grad_out, gain, w_gate, w_up, w_down):
    samp_dev, local_tok, features = tokens.shape
    groups = lax.axis_size("token")
    head_size = features // groups
    hops = moves(lax.axis_size("dp"))
    w_gate, w_up, w_down = w_gate[0], w_up[0], w_down[0]

    def outgoing(source):
        return source.reshape(samp_dev, groups, head_size)

    def exchange(source):
        arrived = lax.all_to_all(outgoing(source), "token", split_axis=1, concat_axis=1, tiled=True)
        return arrived.reshape(samp_dev, features)

    tokens, grad_out = tokens[:, 0], grad_out[:, 0]
    mixed_in = exchange(tokens)
    grads = gather(grad_out, hops)

    summed = tokens.astype(F32) + mixed_in.astype(F32)
    inv_rms = lax.rsqrt(jnp.mean(summed * summed, axis=-1, keepdims=True) + 1e-06)
    normed = summed * inv_rms
    hidden_in = (normed * gain).astype(BF)
    rows = gather(hidden_in, hops)

    acts, d_gates, d_ups, parts = [], [], [], []
    for row, grad in zip(rows, grads):
        gate_out = dot(row, w_gate, ((1,), (0,)))
        up_out = dot(row, w_up, ((1,), (0,)))
        d_activation = dot(grad, w_down, ((1,), (1,)))
        sigmoid_gate = jax.nn.sigmoid(gate_out)
        silu_gate = gate_out * sigmoid_gate
        acts.append((silu_gate * up_out).astype(BF))
        silu_slope = sigmoid_gate * (1.0 + gate_out * (1.0 - sigmoid_gate))
        d_gate_pre = (d_activation * up_out * silu_slope).astype(BF)
        d_up_pre = (d_activation * silu_gate).astype(BF)
        d_gates.append(d_gate_pre)
        d_ups.append(d_up_pre)
        parts.append(dot(d_gate_pre, w_gate, ((1,), (1,))) + dot(d_up_pre, w_up, ((1,), (1,))))

    d_hidden = scatter_sum(parts, samp_dev, hops)

    rows_all, grads_all = cat(*rows), cat(*grads)
    d_w_gate = dot(rows_all, cat(*d_gates), ((0,), (0,)))
    d_w_up = dot(rows_all, cat(*d_ups), ((0,), (0,)))
    d_w_down = dot(cat(*acts), grads_all, ((0,), (0,))).astype(BF)
    gain_part = jnp.sum(d_w_gate * w_gate.astype(F32) + d_w_up * w_up.astype(F32), axis=1)[None] / gain
    d_gain = jnp.sum(lax.all_gather(gain_part, "dp", axis=0, tiled=True), axis=0, keepdims=True)

    scaled = d_hidden * gain
    d_summed = grad_out.astype(F32) + inv_rms * (
        scaled - normed * jnp.mean(scaled * normed, axis=-1, keepdims=True)
    )
    mixed_back = exchange(d_summed.astype(BF)).astype(F32)
    d_tokens = (d_summed + mixed_back).astype(BF)
    return (
        d_tokens[:, None],
        d_w_gate.astype(BF)[None],
        d_w_up.astype(BF)[None],
        d_w_down[None],
        d_gain,
    )


def solution(mesh):
    placed = (
        P("dp", "token", None),
        P("dp", "token", None),
        P("token", None),
        P("token", None, "dp"),
        P("token", None, "dp"),
        P("token", "dp", None),
    )
    return jax.shard_map(
        shards,
        mesh=mesh,
        in_specs=placed,
        out_specs=(
            P("dp", "token", None),
            P("token", None, "dp"),
            P("token", None, "dp"),
            P("token", "dp", None),
            P("token", None),
        ),
        check_vma=False,
    )
```

```python
import jax
import jax.numpy as jnp
from jax import lax
from jax.experimental import pallas as pl
from jax.experimental.pallas import tpu as pltpu
from jax.sharding import PartitionSpec as P

BF = jnp.bfloat16
F32 = jnp.float32
VMEM = 40 * 1024 * 1024
ROWS_IN = ((0,), (0,))
COLUMNS_OUT = ((1,), (0,))
COLUMNS_IN = ((1,), (1,))
HBM = pl.BlockSpec(memory_space=pl.ANY)


def moves(size):
    ring = size // 2

    def at(z, x):
        return (z % ring) * 2 + x

    places = [(z, x) for z in range(ring) for x in range(2)]
    down = [(at(z, x), at(z - 1, x)) for z, x in places]
    rise = [(at(z, x), at(z + 1, x)) for z, x in places]
    swap = [(at(z, x), at(z, 1 - x)) for z, x in places]

    def from_above(block):
        return lax.ppermute(block, "dp", down)

    def from_below(block):
        return lax.ppermute(block, "dp", rise)

    def from_pair(block):
        return lax.ppermute(block, "dp", swap)

    return from_above, from_below, from_pair


def tie(values, others):
    return lax.optimization_barrier((tuple(values), tuple(others)))[0]


def opposite(block, size):
    return lax.ppermute(block, "dp", [(at, (at + size // 2) % size) for at in range(size)])


def dot(a, b, dims):
    return lax.dot_general(a, b, (dims, ((), ())), preferred_element_type=F32)


def kernel(body, shapes, args, name, flops=0, specs=None, scratch=()):
    outs = tuple(jax.ShapeDtypeStruct(shape, kind) for shape, kind in shapes)
    moved = sum(a.size * a.dtype.itemsize for a in args) + sum(o.size * o.dtype.itemsize for o in outs)
    whole = pl.BlockSpec(memory_space=pltpu.VMEM)
    return pl.pallas_call(
        body,
        out_shape=outs,
        in_specs=[whole] * len(args) if specs is None else specs,
        out_specs=tuple(whole for _ in outs),
        scratch_shapes=list(scratch),
        compiler_params=pltpu.CompilerParams(vmem_limit_bytes=VMEM),
        cost_estimate=pl.CostEstimate(flops=flops, bytes_accessed=moved, transcendentals=0),
        name=name,
    )(*args)


def put_heads(ref, whole):
    size = ref.shape[2]
    for head in range(ref.shape[0]):
        ref[head] = whole[:, head * size : (head + 1) * size].astype(BF)


def take_heads(ref):
    return jnp.concatenate([ref[head].astype(F32) for head in range(ref.shape[0])], axis=1)


def split_heads(source, heads):
    rows, features = source.shape

    def body(source_ref, out_ref):
        put_heads(out_ref, source_ref[...].astype(F32))

    return kernel(body, [((heads, rows, features // heads), BF)], [source], "split_heads")[0]


def normalize(arrived, tokens, gain):
    rows, features = tokens.shape

    def body(arrived_ref, tokens_ref, gain_ref, hidden_ref, normed_ref, scale_ref):
        summed = tokens_ref[...].astype(F32) + take_heads(arrived_ref)
        scale = lax.rsqrt(jnp.mean(summed * summed, axis=-1, keepdims=True) + 1e-06)
        normed = summed * scale
        hidden_ref[...] = (normed * gain_ref[...]).astype(BF)
        normed_ref[...] = normed
        scale_ref[...] = jnp.broadcast_to(scale, (rows, 128))

    shapes = [((rows, features), BF), ((rows, features), F32), ((rows, 128), F32)]
    return kernel(body, shapes, [arrived, tokens, gain], "normalize", flops=30 * 10**9)


def token_gradient(own, arrived, straight, grad_out, normed, scale, gain, heads):
    rows, features = grad_out.shape

    def body(own_ref, a_ref, b_ref, c_ref, d_ref, near_ref, grad_ref, normed_ref, scale_ref, gain_ref, sum_ref, heads_ref, total_ref):
        d_hidden = own_ref[...].astype(F32)
        for ref in (a_ref, b_ref, c_ref, d_ref):
            d_hidden = d_hidden + ref[:rows, :].astype(F32)
        scaled = d_hidden * gain_ref[...]
        normed = normed_ref[...]
        mean = jnp.mean(scaled * normed, axis=-1, keepdims=True)
        d_summed = grad_ref[...].astype(F32) + scale_ref[:, :1] * (scaled - normed * mean)
        sum_ref[...] = d_summed
        put_heads(heads_ref, d_summed)
        total = word_sum(near_ref[rows:, :].astype(F32)) + word_sum(d_ref[rows:, :].astype(F32))
        total_ref[...] = total + word_sum(a_ref[rows:, :].astype(F32)) + word_sum(b_ref[rows:, :].astype(F32))

    shapes = [((rows, features), F32), ((heads, rows, features // heads), BF), ((1, features), F32)]
    return kernel(body, shapes, [own, *arrived, straight, grad_out, normed, scale, gain], "token_gradient")


def add_heads(d_summed, arrived):
    def body(sum_ref, arrived_ref, out_ref):
        out_ref[...] = (sum_ref[...] + take_heads(arrived_ref)).astype(BF)

    return kernel(body, [(d_summed.shape, BF)], [d_summed, arrived], "add_heads")[0]


def join_two(one, two):
    rows, features = one.shape

    def body(one_ref, two_ref, out_ref, sems):
        copies = [pltpu.make_async_copy(ref, out_ref.at[pl.ds(at * rows, rows)], sems.at[at]) for at, ref in enumerate((one_ref, two_ref))]
        for copy in copies:
            copy.start()
        for copy in copies:
            copy.wait()

    return kernel(body, [((2 * rows, features), BF)], [one, two], "join_two", flops=20 * 10**9, specs=[HBM] * 2, scratch=[pltpu.SemaphoreType.DMA((2,))])[0]


def feed_forward(blocks, grads, w_gate, w_up, w_down, split=True):
    rows = blocks[0][0].shape[0]
    flat = [block for two in blocks for block in two]
    count = len(flat) * rows
    features, units = w_gate.shape
    half = rows // 2
    alone, paired = len(blocks) % 2, len(blocks) // 2
    n_in = len(flat) + len(grads) + 3

    def body(*refs):
        row_refs, grad_refs = refs[: len(flat)], refs[len(flat) : n_in - 3]
        wg_ref, wu_ref, wd_ref = refs[n_in - 3 : n_in]
        row_ref, grad_ref, act_ref, dg_ref, du_ref, gain_ref = refs[n_in : n_in + 6]
        part_refs = refs[n_in + 6 :]
        for whole, pieces in ((row_ref, row_refs), (grad_ref, grad_refs)):
            at = 0
            for piece in pieces:
                whole[at : at + piece.shape[0], :] = piece[...]
                at += piece.shape[0]
        row = row_ref[...]
        gate_out = dot(row, wg_ref[...], COLUMNS_OUT)
        up_out = dot(row, wu_ref[...], COLUMNS_OUT)
        d_activation = dot(grad_ref[...], wd_ref[...], COLUMNS_IN)
        sigmoid_gate = jax.nn.sigmoid(gate_out)
        silu_gate = gate_out * sigmoid_gate
        act_ref[...] = (silu_gate * up_out).astype(BF)
        silu_slope = sigmoid_gate * (1.0 + gate_out * (1.0 - sigmoid_gate))
        d_gate_pre = (d_activation * up_out * silu_slope).astype(BF)
        d_up_pre = (d_activation * silu_gate).astype(BF)
        dg_ref[...] = d_gate_pre
        du_ref[...] = d_up_pre
        part = dot(d_gate_pre, wg_ref[...], COLUMNS_IN) + dot(d_up_pre, wu_ref[...], COLUMNS_IN)
        gain_ref[...] = jnp.sum(part * row_ref[...].astype(F32), axis=0, keepdims=True)
        part = part.astype(BF)
        at, out = 0, iter(part_refs)
        for _ in range(alone):
            next(out)[...] = part[at : at + rows]
            next(out)[...] = part[at + rows : at + 2 * rows]
            at += 2 * rows
        for _ in range(paired):
            up, up_side, dn, dn_side = (part[at + i * rows : at + (i + 1) * rows] for i in range(4))
            for whole in (up, dn):
                next(out)[...] = whole
            if split:
                for piece in (up_side[:half], dn_side[:half]):
                    next(out)[...] = piece
                up_side, dn_side = up_side[half:], dn_side[half:]
            sides = next(out)
            sides[: up_side.shape[0]] = up_side
            sides[up_side.shape[0] :] = dn_side
            at += 4 * rows

    wide, thin, piece, short = ((count, features), BF), ((count, units), BF), ((rows, features), BF), ((half, features), BF)
    shapes = [wide, wide, thin, thin, thin, ((1, features), F32)] + [piece] * (2 * alone) + ([piece, piece, short, short, piece] if split else [piece, piece, ((2 * rows, features), BF)]) * paired
    return kernel(body, shapes, [*flat, *grads, w_gate, w_up, w_down], "feed_forward", flops=10 * count * features * units)


def two_words(value):
    high = value.astype(BF).astype(F32)
    at = lax.broadcasted_iota(jnp.int32, (16, value.shape[1]), 0)
    return jnp.where(at == 0, high, jnp.where(at == 1, value - high, 0.0))


def word_sum(rows):
    return jnp.sum(rows, axis=0, keepdims=True)


def add_step(step, args, widths):
    features = args[0].shape[1]
    count = len(args)

    def body(*refs):
        for out, parts in zip(refs[count:], step([ref[...].astype(F32) for ref in refs[:count]])):
            at = 0
            for part in parts:
                out[at : at + part.shape[0], :] = part.astype(BF)
                at += part.shape[0]

    return kernel(body, [((width, features), BF) for width in widths], args, "add_step")


def weight_gradient(lefts, rights, name):
    count, shape = len(lefts), (lefts[0].shape[1], rights[0].shape[1])

    def body(*refs):
        total = dot(refs[0][...], refs[count][...], ROWS_IN)
        for at in range(1, count):
            total = total + dot(refs[at][...], refs[count + at][...], ROWS_IN)
        refs[-1][...] = total.astype(BF)

    rows = sum(left.shape[0] for left in lefts)
    return kernel(body, [(shape, BF)], [*lefts, *rights], name, flops=2 * rows * shape[0] * shape[1])[0]


def shards(tokens, grad_out, gain, w_gate, w_up, w_down):
    rows = tokens.shape[0]
    half = rows // 2
    wide = rows + half
    heads, size = lax.axis_size("token"), lax.axis_size("dp")
    above, below, pair = moves(size)
    w_gate, w_up, w_down = w_gate[0], w_up[0], w_down[0]

    def exchange(blocks):
        return lax.all_to_all(blocks, "token", split_axis=0, concat_axis=0, tiled=True)

    tokens, grad_out = tokens[:, 0], grad_out[:, 0]
    g_s0 = pair(grad_out)
    mixed_in = exchange(split_heads(tokens, heads))
    hidden_in, normed, scale = normalize(mixed_in, tokens, gain)
    g0 = join_two(grad_out, g_s0)

    u1, d1, s0 = above(hidden_in), below(hidden_in), pair(hidden_in)
    g_u1, g_d1 = above(g0), below(g0)
    u2, d2, s_u1, s_d1 = above(u1), below(d1), pair(u1), pair(d1)
    g_u2, g_d2 = above(g_u1), below(g_d1)
    u2, d2 = tie([u2, d2], [s0])
    u3, d3, s_u2, s_d2 = above(u2), below(d2), pair(u2), pair(d2)
    g_u3, g_d3 = above(g_u2), below(g_d2)
    u3, d3 = tie([u3, d3], [s_u1, s_d1, s_u2, s_d2])
    s_u3, s_d3, far = pair(u3), pair(d3), below(d3)
    g_far = above(g_u3)
    near = feed_forward([(hidden_in, s0), (u1, s_u1), (d1, s_d1)], [g0, g_u1, g_d1], w_gate, w_up, w_down)
    second = feed_forward([(u2, s_u2), (d2, s_d2)], [g_u2, g_d2], w_gate, w_up, w_down)
    s_u3, s_d3 = tie([s_u3, s_d3], [near[6], second[6], far])
    third = feed_forward([(u3, s_u3), (d3, s_d3)], [g_u3, g_d3], w_gate, w_up, w_down, split=False)

    own, own_side, p_u1, p_d1, low_u1, low_d1, high1 = near[6:]
    p_u2, p_d2, low_u2, low_d2, high2 = second[6:]
    p_u3, p_d3, side3 = third[6:]

    def first_sums(v):
        c, up, dn, up_low, dn_low = v
        return [(up + c[:rows], up_low), (dn + c[rows:], dn_low)]

    def second_sums(v):
        a, b, c, up, dn, up_low, dn_low, one, two = v
        spare = two_words(one + two)
        go_up = (up[:half] + a[:half], up[half:] + a[half:rows] + c[:half], up_low + a[rows:], spare)
        go_dn = (dn[:half] + b[:half], dn[half:] + b[half:rows] + c[half:], dn_low + b[rows:], spare)
        return [go_up, go_dn]

    def last_sums(v):
        a, b, c, up, dn, side, p_far, got, one, two = v
        go_up = (up[:half] + a[:half], up[half:] + a[half:rows] + c[:half], a[wide:])
        go_dn = (dn[:half] + b[:half], dn[half:] + b[half:rows] + c[half:], b[wide:])
        around = two_words(one + two + word_sum(a[wide:]) + word_sum(b[wide:]))
        return [go_up, go_dn, (side[:half] + a[rows:wide] + b[rows:wide], side[half:]), (p_far + got, around)]

    c, s_far = pair(side3), pair(far)
    go_up, go_dn = add_step(first_sums, [c, p_u3, p_d3, low_u2, low_d2], (wide, wide))
    a, b, c = below(go_up), above(go_dn), pair(high2)
    (s_far,) = tie([s_far], [go_up])
    fourth = feed_forward([(far, s_far)], [g_far], w_gate, w_up, w_down)
    groups = (near, second, third, fourth)
    part = sum(group[5] for group in groups) / gain
    part_side = pair(part)
    d_w_down = weight_gradient([group[2] for group in groups], [group[1] for group in groups], "d_w_down")
    a, b, c = tie([a, b, c], [part_side, d_w_down])
    go_up, go_dn = add_step(second_sums, [a, b, c, p_u2, p_d2, low_u1, low_d1, part, part_side], (wide + 16, wide + 16))
    p_far, p_far_side = fourth[6:]
    a, b, c, got = below(go_up), above(go_dn), pair(high1), pair(p_far_side)
    row_parts = tie([group[0] for group in groups], [go_up])
    d_w_gate = weight_gradient(row_parts, [group[3] for group in groups], "d_w_gate")
    a, b, c = tie([a, b, c], [got, d_w_gate])
    go_up, go_dn, go_side, straight = add_step(
        last_sums, [a, b, c, p_u1, p_d1, own_side, p_far, got, part, part_side], (rows + 16, rows + 16, rows, rows + 16)
    )
    row_parts = tie([group[0] for group in groups], [go_up])
    d_w_up = weight_gradient(row_parts, [group[4] for group in groups], "d_w_up")
    arrived = tie([below(go_up), above(go_dn), pair(go_side), opposite(straight, size)], [d_w_up])

    d_summed, outgoing, d_gain = token_gradient(own, arrived, straight, grad_out, normed, scale, gain, heads)
    d_tokens = add_heads(d_summed, exchange(outgoing))
    return d_tokens[:, None], d_w_gate[None], d_w_up[None], d_w_down[None], d_gain


def solution(mesh):
    placed = (
        P("dp", "token", None),
        P("dp", "token", None),
        P("token", None),
        P("token", None, "dp"),
        P("token", None, "dp"),
        P("token", "dp", None),
    )
    return jax.shard_map(
        shards,
        mesh=mesh,
        in_specs=placed,
        out_specs=(
            P("dp", "token", None),
            P("token", None, "dp"),
            P("token", None, "dp"),
            P("token", "dp", None),
            P("token", None),
        ),
        check_vma=False,
    )
```

```python
import jax
import jax.numpy as jnp
from jax import lax
from jax.experimental import pallas as pl
from jax.experimental.pallas import tpu as pltpu
from jax.sharding import PartitionSpec as P

BF = jnp.bfloat16
F32 = jnp.float32
VMEM = 40 * 1024 * 1024
ROWS_IN = ((0,), (0,))
COLUMNS_OUT = ((1,), (0,))
COLUMNS_IN = ((1,), (1,))
HBM = pl.BlockSpec(memory_space=pl.ANY)


def moves(size):
    ring = size // 2

    def at(z, x):
        return (z % ring) * 2 + x

    places = [(z, x) for z in range(ring) for x in range(2)]
    down = [(at(z, x), at(z - 1, x)) for z, x in places]
    rise = [(at(z, x), at(z + 1, x)) for z, x in places]
    swap = [(at(z, x), at(z, 1 - x)) for z, x in places]

    def from_above(block):
        return lax.ppermute(block, "dp", down)

    def from_below(block):
        return lax.ppermute(block, "dp", rise)

    def from_pair(block):
        return lax.ppermute(block, "dp", swap)

    return from_above, from_below, from_pair


def tie(values, others):
    return lax.optimization_barrier((tuple(values), tuple(others)))[0]


def opposite(block, size):
    return lax.ppermute(block, "dp", [(at, (at + size // 2) % size) for at in range(size)])


def dot(a, b, dims):
    return lax.dot_general(a, b, (dims, ((), ())), preferred_element_type=F32)


def kernel(body, shapes, args, name, flops=0, specs=None, scratch=()):
    outs = tuple(jax.ShapeDtypeStruct(shape, kind) for shape, kind in shapes)
    moved = sum(a.size * a.dtype.itemsize for a in args) + sum(o.size * o.dtype.itemsize for o in outs)
    whole = pl.BlockSpec(memory_space=pltpu.VMEM)
    return pl.pallas_call(
        body,
        out_shape=outs,
        in_specs=[whole] * len(args) if specs is None else specs,
        out_specs=tuple(whole for _ in outs),
        scratch_shapes=list(scratch),
        compiler_params=pltpu.CompilerParams(vmem_limit_bytes=VMEM),
        cost_estimate=pl.CostEstimate(flops=flops, bytes_accessed=moved, transcendentals=0),
        name=name,
    )(*args)


def put_heads(ref, whole):
    size = ref.shape[2]
    for head in range(ref.shape[0]):
        ref[head] = whole[:, head * size : (head + 1) * size].astype(BF)


def take_heads(ref):
    return jnp.concatenate([ref[head].astype(F32) for head in range(ref.shape[0])], axis=1)


def split_heads(source, heads):
    rows, features = source.shape

    def body(source_ref, out_ref):
        put_heads(out_ref, source_ref[...].astype(F32))

    return kernel(body, [((heads, rows, features // heads), BF)], [source], "split_heads")[0]


def normalize(arrived, tokens, gain):
    rows, features = tokens.shape

    def body(arrived_ref, tokens_ref, gain_ref, hidden_ref, normed_ref, scale_ref):
        summed = tokens_ref[...].astype(F32) + take_heads(arrived_ref)
        scale = lax.rsqrt(jnp.mean(summed * summed, axis=-1, keepdims=True) + 1e-06)
        normed = summed * scale
        hidden_ref[...] = (normed * gain_ref[...]).astype(BF)
        normed_ref[...] = normed
        scale_ref[...] = jnp.broadcast_to(scale, (rows, 128))

    shapes = [((rows, features), BF), ((rows, features), F32), ((rows, 128), F32)]
    return kernel(body, shapes, [arrived, tokens, gain], "normalize", flops=30 * 10**9)


def token_gradient(own, arrived, around, grad_out, normed, scale, gain, heads):
    rows, features = grad_out.shape

    def body(own_ref, a_ref, b_ref, c_ref, d_ref, near_ref, grad_ref, normed_ref, scale_ref, gain_ref, sum_ref, heads_ref, total_ref):
        d_hidden = own_ref[...].astype(F32)
        for ref in (a_ref, b_ref, c_ref, d_ref):
            d_hidden = d_hidden + ref[:rows, :].astype(F32)
        scaled = d_hidden * gain_ref[...]
        normed = normed_ref[...]
        mean = jnp.mean(scaled * normed, axis=-1, keepdims=True)
        d_summed = grad_ref[...].astype(F32) + scale_ref[:, :1] * (scaled - normed * mean)
        sum_ref[...] = d_summed
        put_heads(heads_ref, d_summed)
        total_ref[...] = near_ref[...] + word_sum(a_ref[rows:, :].astype(F32)) + word_sum(b_ref[rows:, :].astype(F32))

    shapes = [((rows, features), F32), ((heads, rows, features // heads), BF), ((1, features), F32)]
    return kernel(body, shapes, [own, *arrived, around, grad_out, normed, scale, gain], "token_gradient")


def total_gain(one, two):
    def body(one_ref, two_ref, out_ref):
        out_ref[...] = one_ref[...] + two_ref[...]

    return kernel(body, [(one.shape, F32)], [one, two], "total_gain", flops=10**9)[0]


def add_heads(d_summed, arrived):
    def body(sum_ref, arrived_ref, out_ref):
        out_ref[...] = (sum_ref[...] + take_heads(arrived_ref)).astype(BF)

    return kernel(body, [(d_summed.shape, BF)], [d_summed, arrived], "add_heads")[0]


def join_two(one, two):
    rows, features = one.shape

    def body(one_ref, two_ref, out_ref, sems):
        copies = [pltpu.make_async_copy(ref, out_ref.at[pl.ds(at * rows, rows)], sems.at[at]) for at, ref in enumerate((one_ref, two_ref))]
        for copy in copies:
            copy.start()
        for copy in copies:
            copy.wait()

    return kernel(body, [((2 * rows, features), BF)], [one, two], "join_two", flops=20 * 10**9, specs=[HBM] * 2, scratch=[pltpu.SemaphoreType.DMA((2,))])[0]


def feed_forward(blocks, grads, w_gate, w_up, w_down):
    rows = blocks[0][0].shape[0]
    flat = [block for two in blocks for block in two]
    count = len(flat) * rows
    features, units = w_gate.shape
    half = rows // 2
    alone, paired = len(blocks) % 2, len(blocks) // 2
    n_in = len(flat) + len(grads) + 3

    def body(*refs):
        row_refs, grad_refs = refs[: len(flat)], refs[len(flat) : n_in - 3]
        wg_ref, wu_ref, wd_ref = refs[n_in - 3 : n_in]
        row_ref, grad_ref, act_ref, dg_ref, du_ref, gain_ref = refs[n_in : n_in + 6]
        part_refs = refs[n_in + 6 :]
        for whole, pieces in ((row_ref, row_refs), (grad_ref, grad_refs)):
            at = 0
            for piece in pieces:
                whole[at : at + piece.shape[0], :] = piece[...]
                at += piece.shape[0]
        row = row_ref[...]
        gate_out = dot(row, wg_ref[...], COLUMNS_OUT)
        up_out = dot(row, wu_ref[...], COLUMNS_OUT)
        d_activation = dot(grad_ref[...], wd_ref[...], COLUMNS_IN)
        sigmoid_gate = jax.nn.sigmoid(gate_out)
        silu_gate = gate_out * sigmoid_gate
        act_ref[...] = (silu_gate * up_out).astype(BF)
        silu_slope = sigmoid_gate * (1.0 + gate_out * (1.0 - sigmoid_gate))
        d_gate_pre = (d_activation * up_out * silu_slope).astype(BF)
        d_up_pre = (d_activation * silu_gate).astype(BF)
        dg_ref[...] = d_gate_pre
        du_ref[...] = d_up_pre
        part = dot(d_gate_pre, wg_ref[...], COLUMNS_IN) + dot(d_up_pre, wu_ref[...], COLUMNS_IN)
        gain_ref[...] = jnp.sum(part * row_ref[...].astype(F32), axis=0, keepdims=True)
        part = part.astype(BF)
        at, out = 0, iter(part_refs)
        for _ in range(alone):
            next(out)[...] = part[at : at + rows]
            next(out)[...] = part[at + rows : at + 2 * rows]
            at += 2 * rows
        for _ in range(paired):
            up, up_side, dn, dn_side = (part[at + i * rows : at + (i + 1) * rows] for i in range(4))
            for whole in (up, dn):
                next(out)[...] = whole
            for piece in (up_side[:half], dn_side[:half]):
                next(out)[...] = piece
            high = next(out)
            high[:half] = up_side[half:]
            high[half:] = dn_side[half:]
            at += 4 * rows

    wide, thin, piece, short = ((count, features), BF), ((count, units), BF), ((rows, features), BF), ((half, features), BF)
    shapes = [wide, wide, thin, thin, thin, ((1, features), F32)] + [piece] * (2 * alone) + [piece, piece, short, short, piece] * paired
    return kernel(body, shapes, [*flat, *grads, w_gate, w_up, w_down], "feed_forward", flops=10 * count * features * units)


def two_words(value):
    high = value.astype(BF).astype(F32)
    at = lax.broadcasted_iota(jnp.int32, (16, value.shape[1]), 0)
    return jnp.where(at == 0, high, jnp.where(at == 1, value - high, 0.0))


def word_sum(rows):
    return jnp.sum(rows, axis=0, keepdims=True)


def add_step(step, args, widths):
    features = args[0].shape[1]
    count = len(args)

    def body(*refs):
        for out, parts in zip(refs[count:], step([ref[...].astype(F32) for ref in refs[:count]])):
            at = 0
            for part in parts:
                out[at : at + part.shape[0], :] = part.astype(out.dtype)
                at += part.shape[0]

    shapes = [((1, features), F32) if width is F32 else ((width, features), BF) for width in widths]
    return kernel(body, shapes, args, "add_step")


def weight_gradient(lefts, rights, name):
    count, shape = len(lefts), (lefts[0].shape[1], rights[0].shape[1])

    def body(*refs):
        total = dot(refs[0][...], refs[count][...], ROWS_IN)
        for at in range(1, count):
            total = total + dot(refs[at][...], refs[count + at][...], ROWS_IN)
        refs[-1][...] = total.astype(BF)

    rows = sum(left.shape[0] for left in lefts)
    return kernel(body, [(shape, BF)], [*lefts, *rights], name, flops=2 * rows * shape[0] * shape[1])[0]


def shards(tokens, grad_out, gain, w_gate, w_up, w_down):
    rows = tokens.shape[0]
    half = rows // 2
    wide = rows + half
    heads, size = lax.axis_size("token"), lax.axis_size("dp")
    above, below, pair = moves(size)
    w_gate, w_up, w_down = w_gate[0], w_up[0], w_down[0]

    def exchange(blocks):
        return lax.all_to_all(blocks, "token", split_axis=0, concat_axis=0, tiled=True)

    tokens, grad_out = tokens[:, 0], grad_out[:, 0]
    g_s0 = pair(grad_out)
    mixed_in = exchange(split_heads(tokens, heads))
    hidden_in, normed, scale = normalize(mixed_in, tokens, gain)
    g0 = join_two(grad_out, g_s0)

    u1, d1, s0 = above(hidden_in), below(hidden_in), pair(hidden_in)
    g_u1, g_d1 = above(g0), below(g0)
    u2, d2, s_u1, s_d1 = above(u1), below(d1), pair(u1), pair(d1)
    g_u2, g_d2 = above(g_u1), below(g_d1)
    u2, d2 = tie([u2, d2], [s0])
    u3, d3, s_u2, s_d2 = above(u2), below(d2), pair(u2), pair(d2)
    g_u3, g_d3 = above(g_u2), below(g_d2)
    u3, d3 = tie([u3, d3], [s_u1, s_d1, s_u2, s_d2])
    s_u3, s_d3, far = pair(u3), pair(d3), below(d3)
    g_far = above(g_u3)
    near = feed_forward([(hidden_in, s0), (u1, s_u1), (d1, s_d1)], [g0, g_u1, g_d1], w_gate, w_up, w_down)
    second = feed_forward([(u2, s_u2), (d2, s_d2)], [g_u2, g_d2], w_gate, w_up, w_down)
    s_u3, s_d3 = tie([s_u3, s_d3], [near[6], second[6], far])
    third = feed_forward([(u3, s_u3), (d3, s_d3)], [g_u3, g_d3], w_gate, w_up, w_down)

    own, own_side, p_u1, p_d1, low_u1, low_d1, high1 = near[6:]
    p_u2, p_d2, low_u2, low_d2, high2 = second[6:]
    p_u3, p_d3, low_u3, low_d3, high3 = third[6:]

    def first_sums(v):
        a, b, c, up, dn, up_low, dn_low = v
        return [(up[:half], up[half:] + c[:half], up_low + a), (dn[:half], dn[half:] + c[half:], dn_low + b)]

    def second_sums(v):
        a, b, c, up, dn, up_low, dn_low, p_far, got, one, two = v
        spare = two_words(one + two)
        go_up = (up[:half] + a[:half], up[half:] + a[half:rows] + c[:half], up_low + a[rows:], spare)
        go_dn = (dn[:half] + b[:half], dn[half:] + b[half:rows] + c[half:], dn_low + b[rows:], spare)
        return [go_up, go_dn, (p_far + got,)]

    def last_sums(v):
        a, b, c, up, dn, side, one, two = v
        go_up = (up[:half] + a[:half], up[half:] + a[half:rows] + c[:half], a[wide:])
        go_dn = (dn[:half] + b[:half], dn[half:] + b[half:rows] + c[half:], b[wide:])
        around = one + two + word_sum(a[wide:]) + word_sum(b[wide:])
        return [go_up, go_dn, (side[:half] + a[rows:wide] + b[rows:wide], side[half:]), (around,)]

    a, b, c, s_far = below(low_u3), above(low_d3), pair(high3), pair(far)
    go_up, go_dn = add_step(first_sums, [a, b, c, p_u3, p_d3, low_u2, low_d2], (wide, wide))
    a, b, c = below(go_up), above(go_dn), pair(high2)
    (s_far,) = tie([s_far], [go_up])
    fourth = feed_forward([(far, s_far)], [g_far], w_gate, w_up, w_down)
    groups = (near, second, third, fourth)
    part = sum(group[5] for group in groups) / gain
    p_far, p_far_side = fourth[6:]
    part_side, got = pair(part), pair(p_far_side)
    d_w_down = weight_gradient([group[2] for group in groups], [group[1] for group in groups], "d_w_down")
    a, b, c = tie([a, b, c], [part_side, got, d_w_down])
    sums = [a, b, c, p_u2, p_d2, low_u1, low_d1, p_far, got, part, part_side]
    go_up, go_dn, straight = add_step(second_sums, sums, (wide + 16, wide + 16, rows))
    a, b, c = below(go_up), above(go_dn), pair(high1)
    row_parts = tie([group[0] for group in groups], [go_up])
    d_w_gate = weight_gradient(row_parts, [group[3] for group in groups], "d_w_gate")
    a, b, c = tie([a, b, c], [d_w_gate])
    sums = [a, b, c, p_u1, p_d1, own_side, part, part_side]
    go_up, go_dn, go_side, around = add_step(last_sums, sums, (rows + 16, rows + 16, rows, F32))
    straight = opposite(straight, size)
    row_parts = tie([group[0] for group in groups], [go_up, straight])
    d_w_up = weight_gradient(row_parts, [group[4] for group in groups], "d_w_up")
    arrived = tie([below(go_up), above(go_dn), pair(go_side), straight], [d_w_up])

    d_summed, outgoing, five = token_gradient(own, arrived, around, grad_out, normed, scale, gain, heads)
    (around,) = tie([around], [outgoing])
    d_gain = total_gain(five, opposite(around, size))
    d_tokens = add_heads(d_summed, exchange(outgoing))
    return d_tokens[:, None], d_w_gate[None], d_w_up[None], d_w_down[None], d_gain


def solution(mesh):
    placed = (
        P("dp", "token", None),
        P("dp", "token", None),
        P("token", None),
        P("token", None, "dp"),
        P("token", None, "dp"),
        P("token", "dp", None),
    )
    return jax.shard_map(
        shards,
        mesh=mesh,
        in_specs=placed,
        out_specs=(
            P("dp", "token", None),
            P("token", None, "dp"),
            P("token", None, "dp"),
            P("token", "dp", None),
            P("token", None),
        ),
        check_vma=False,
    )
```

```python
import jax
import jax.numpy as jnp
from jax import lax
from jax.experimental import pallas as pl
from jax.experimental.pallas import tpu as pltpu
from jax.sharding import PartitionSpec as P

BF = jnp.bfloat16
F32 = jnp.float32
VMEM = 40 * 1024 * 1024
ROWS_IN = ((0,), (0,))
COLUMNS_OUT = ((1,), (0,))
COLUMNS_IN = ((1,), (1,))
HBM = pl.BlockSpec(memory_space=pl.ANY)


def moves(size):
    ring = size // 2

    def swap(partner):
        pairs = [(z * 2 + x, (partner(z) % ring) * 2 + x) for z in range(ring) for x in range(2)]
        return lambda block: lax.ppermute(block, "dp", pairs)

    first = swap(lambda z: z + 1 if z % 2 == 0 else z - 1)
    other = swap(lambda z: z - 1 if z % 2 == 0 else z + 1)
    return first, other, lambda block: lax.ppermute(block, "dp", [(at, at ^ 1) for at in range(size)])


def tie(values, others):
    return lax.optimization_barrier((tuple(values), tuple(others)))[0]


def opposite(block, size):
    return lax.ppermute(block, "dp", [(at, (at + size // 2) % size) for at in range(size)])


def dot(a, b, dims):
    return lax.dot_general(a, b, (dims, ((), ())), preferred_element_type=F32)


def kernel(body, shapes, args, name, flops=0, specs=None, scratch=()):
    outs = tuple(jax.ShapeDtypeStruct(shape, kind) for shape, kind in shapes)
    moved = sum(a.size * a.dtype.itemsize for a in args) + sum(o.size * o.dtype.itemsize for o in outs)
    whole = pl.BlockSpec(memory_space=pltpu.VMEM)
    return pl.pallas_call(
        body,
        out_shape=outs,
        in_specs=[whole] * len(args) if specs is None else specs,
        out_specs=tuple(whole for _ in outs),
        scratch_shapes=list(scratch),
        compiler_params=pltpu.CompilerParams(vmem_limit_bytes=VMEM),
        cost_estimate=pl.CostEstimate(flops=flops, bytes_accessed=moved, transcendentals=0),
        name=name,
    )(*args)


def put_heads(ref, whole):
    size = ref.shape[2]
    for head in range(ref.shape[0]):
        ref[head] = whole[:, head * size : (head + 1) * size].astype(BF)


def take_heads(ref):
    return jnp.concatenate([ref[head].astype(F32) for head in range(ref.shape[0])], axis=1)


def split_heads(source, heads):
    rows, features = source.shape

    def body(source_ref, out_ref):
        put_heads(out_ref, source_ref[...].astype(F32))

    return kernel(body, [((heads, rows, features // heads), BF)], [source], "split_heads")[0]


def normalize(arrived, tokens, gain):
    rows, features = tokens.shape

    def body(arrived_ref, tokens_ref, gain_ref, hidden_ref, normed_ref, scale_ref):
        summed = tokens_ref[...].astype(F32) + take_heads(arrived_ref)
        scale = lax.rsqrt(jnp.mean(summed * summed, axis=-1, keepdims=True) + 1e-06)
        normed = summed * scale
        hidden_ref[...] = (normed * gain_ref[...]).astype(BF)
        normed_ref[...] = normed
        scale_ref[...] = jnp.broadcast_to(scale, (rows, 128))

    shapes = [((rows, features), BF), ((rows, features), F32), ((rows, 128), F32)]
    return kernel(body, shapes, [arrived, tokens, gain], "normalize", flops=30 * 10**9)


def token_gradient(own, arrived, around, grad_out, normed, scale, gain, heads):
    rows, features = grad_out.shape

    def body(own_ref, a_ref, b_ref, c_ref, d_ref, near_ref, grad_ref, normed_ref, scale_ref, gain_ref, sum_ref, heads_ref, total_ref):
        d_hidden = own_ref[...].astype(F32)
        for ref in (a_ref, b_ref, c_ref, d_ref):
            d_hidden = d_hidden + ref[:rows, :].astype(F32)
        scaled = d_hidden * gain_ref[...]
        normed = normed_ref[...]
        mean = jnp.mean(scaled * normed, axis=-1, keepdims=True)
        d_summed = grad_ref[...].astype(F32) + scale_ref[:, :1] * (scaled - normed * mean)
        sum_ref[...] = d_summed
        put_heads(heads_ref, d_summed)
        total_ref[...] = near_ref[...] + word_sum(a_ref[rows:, :].astype(F32)) + word_sum(b_ref[rows:, :].astype(F32))

    shapes = [((rows, features), F32), ((heads, rows, features // heads), BF), ((1, features), F32)]
    return kernel(body, shapes, [own, *arrived, around, grad_out, normed, scale, gain], "token_gradient")


def total_gain(one, two):
    def body(one_ref, two_ref, out_ref):
        out_ref[...] = one_ref[...] + two_ref[...]

    return kernel(body, [(one.shape, F32)], [one, two], "total_gain", flops=10**9)[0]


def add_heads(d_summed, arrived):
    def body(sum_ref, arrived_ref, out_ref):
        out_ref[...] = (sum_ref[...] + take_heads(arrived_ref)).astype(BF)

    return kernel(body, [(d_summed.shape, BF)], [d_summed, arrived], "add_heads")[0]


def join_two(one, two):
    rows, features = one.shape

    def body(one_ref, two_ref, out_ref, sems):
        copies = [pltpu.make_async_copy(ref, out_ref.at[pl.ds(at * rows, rows)], sems.at[at]) for at, ref in enumerate((one_ref, two_ref))]
        for copy in copies:
            copy.start()
        for copy in copies:
            copy.wait()

    return kernel(body, [((2 * rows, features), BF)], [one, two], "join_two", flops=20 * 10**9, specs=[HBM] * 2, scratch=[pltpu.SemaphoreType.DMA((2,))])[0]


def feed_forward(blocks, grads, w_gate, w_up, w_down):
    rows = blocks[0][0].shape[0]
    flat = [block for two in blocks for block in two]
    count = len(flat) * rows
    features, units = w_gate.shape
    half = rows // 2
    alone, paired = len(blocks) % 2, len(blocks) // 2
    n_in = len(flat) + len(grads) + 3

    def body(*refs):
        row_refs, grad_refs = refs[: len(flat)], refs[len(flat) : n_in - 3]
        wg_ref, wu_ref, wd_ref = refs[n_in - 3 : n_in]
        row_ref, grad_ref, act_ref, dg_ref, du_ref, gain_ref = refs[n_in : n_in + 6]
        part_refs = refs[n_in + 6 :]
        for whole, pieces in ((row_ref, row_refs), (grad_ref, grad_refs)):
            at = 0
            for piece in pieces:
                whole[at : at + piece.shape[0], :] = piece[...]
                at += piece.shape[0]
        row = row_ref[...]
        gate_out = dot(row, wg_ref[...], COLUMNS_OUT)
        up_out = dot(row, wu_ref[...], COLUMNS_OUT)
        d_activation = dot(grad_ref[...], wd_ref[...], COLUMNS_IN)
        sigmoid_gate = jax.nn.sigmoid(gate_out)
        silu_gate = gate_out * sigmoid_gate
        act_ref[...] = (silu_gate * up_out).astype(BF)
        silu_slope = sigmoid_gate * (1.0 + gate_out * (1.0 - sigmoid_gate))
        d_gate_pre = (d_activation * up_out * silu_slope).astype(BF)
        d_up_pre = (d_activation * silu_gate).astype(BF)
        dg_ref[...] = d_gate_pre
        du_ref[...] = d_up_pre
        part = dot(d_gate_pre, wg_ref[...], COLUMNS_IN) + dot(d_up_pre, wu_ref[...], COLUMNS_IN)
        gain_ref[...] = jnp.sum(part * row_ref[...].astype(F32), axis=0, keepdims=True)
        part = part.astype(BF)
        at, out = 0, iter(part_refs)
        for _ in range(alone):
            next(out)[...] = part[at : at + rows]
            next(out)[...] = part[at + rows : at + 2 * rows]
            at += 2 * rows
        for _ in range(paired):
            up, up_side, dn, dn_side = (part[at + i * rows : at + (i + 1) * rows] for i in range(4))
            for whole in (up, dn):
                next(out)[...] = whole
            for piece in (up_side[:half], dn_side[:half]):
                next(out)[...] = piece
            high = next(out)
            high[:half] = up_side[half:]
            high[half:] = dn_side[half:]
            at += 4 * rows

    wide, thin, piece, short = ((count, features), BF), ((count, units), BF), ((rows, features), BF), ((half, features), BF)
    shapes = [wide, wide, thin, thin, thin, ((1, features), F32)] + [piece] * (2 * alone) + [piece, piece, short, short, piece] * paired
    return kernel(body, shapes, [*flat, *grads, w_gate, w_up, w_down], "feed_forward", flops=10 * count * features * units)


def two_words(value):
    high = value.astype(BF).astype(F32)
    at = lax.broadcasted_iota(jnp.int32, (16, value.shape[1]), 0)
    return jnp.where(at == 0, high, jnp.where(at == 1, value - high, 0.0))


def word_sum(rows):
    return jnp.sum(rows, axis=0, keepdims=True)


def add_step(step, args, widths):
    features = args[0].shape[1]
    count = len(args)

    def body(*refs):
        for out, parts in zip(refs[count:], step([ref[...].astype(F32) for ref in refs[:count]])):
            at = 0
            for part in parts:
                out[at : at + part.shape[0], :] = part.astype(out.dtype)
                at += part.shape[0]

    shapes = [((1, features), F32) if width is F32 else ((width, features), BF) for width in widths]
    return kernel(body, shapes, args, "add_step")


def weight_gradient(lefts, rights, name):
    count, shape = len(lefts), (lefts[0].shape[1], rights[0].shape[1])

    def body(*refs):
        total = dot(refs[0][...], refs[count][...], ROWS_IN)
        for at in range(1, count):
            total = total + dot(refs[at][...], refs[count + at][...], ROWS_IN)
        refs[-1][...] = total.astype(BF)

    rows = sum(left.shape[0] for left in lefts)
    return kernel(body, [(shape, BF)], [*lefts, *rights], name, flops=2 * rows * shape[0] * shape[1])[0]


def shards(tokens, grad_out, gain, w_gate, w_up, w_down):
    rows = tokens.shape[0]
    half = rows // 2
    wide = rows + half
    heads, size = lax.axis_size("token"), lax.axis_size("dp")
    first, other, pair = moves(size)
    w_gate, w_up, w_down = w_gate[0], w_up[0], w_down[0]

    def exchange(blocks):
        return lax.all_to_all(blocks, "token", split_axis=0, concat_axis=0, tiled=True)

    tokens, grad_out = tokens[:, 0], grad_out[:, 0]
    g_s0 = pair(grad_out)
    mixed_in = exchange(split_heads(tokens, heads))
    hidden_in, normed, scale = normalize(mixed_in, tokens, gain)
    g0 = join_two(grad_out, g_s0)

    u1, d1, s0 = first(hidden_in), other(hidden_in), pair(hidden_in)
    g_u1, g_d1 = first(g0), other(g0)
    u2, d2, s_u1, s_d1 = first(d1), other(u1), pair(u1), pair(d1)
    g_u2, g_d2 = first(g_d1), other(g_u1)
    u2, d2 = tie([u2, d2], [s0])
    u3, d3, s_u2, s_d2 = first(d2), other(u2), pair(u2), pair(d2)
    g_u3, g_d3 = first(g_d2), other(g_u2)
    u3, d3 = tie([u3, d3], [s_u1, s_d1, s_u2, s_d2])
    s_u3, s_d3, far = pair(u3), pair(d3), first(d3)
    g_far = other(g_u3)
    near = feed_forward([(hidden_in, s0), (u1, s_u1), (d1, s_d1)], [g0, g_u1, g_d1], w_gate, w_up, w_down)
    second = feed_forward([(u2, s_u2), (d2, s_d2)], [g_u2, g_d2], w_gate, w_up, w_down)
    s_u3, s_d3 = tie([s_u3, s_d3], [near[6], second[6], far])
    third = feed_forward([(u3, s_u3), (d3, s_d3)], [g_u3, g_d3], w_gate, w_up, w_down)

    own, own_side, p_u1, p_d1, low_u1, low_d1, high1 = near[6:]
    p_u2, p_d2, low_u2, low_d2, high2 = second[6:]
    p_u3, p_d3, low_u3, low_d3, high3 = third[6:]

    def first_sums(v):
        a, b, c, up, dn, up_low, dn_low = v
        return [(up[:half], up[half:] + c[:half], up_low + a), (dn[:half], dn[half:] + c[half:], dn_low + b)]

    def second_sums(v):
        a, b, c, up, dn, up_low, dn_low, p_far, got, one, two = v
        spare = two_words(one + two)
        go_up = (up[:half] + a[:half], up[half:] + a[half:rows] + c[:half], up_low + a[rows:], spare)
        go_dn = (dn[:half] + b[:half], dn[half:] + b[half:rows] + c[half:], dn_low + b[rows:], spare)
        return [go_up, go_dn, (p_far + got,)]

    def last_sums(v):
        a, b, c, up, dn, side, one, two = v
        go_up = (up[:half] + a[:half], up[half:] + a[half:rows] + c[:half], a[wide:])
        go_dn = (dn[:half] + b[:half], dn[half:] + b[half:rows] + c[half:], b[wide:])
        around = one + two + word_sum(a[wide:]) + word_sum(b[wide:])
        return [go_up, go_dn, (side[:half] + a[rows:wide] + b[rows:wide], side[half:]), (around,)]

    a, b, c, s_far = other(low_d3), first(low_u3), pair(high3), pair(far)
    go_up, go_dn = add_step(first_sums, [a, b, c, p_u3, p_d3, low_u2, low_d2], (wide, wide))
    a, b, c = other(go_dn), first(go_up), pair(high2)
    (s_far,) = tie([s_far], [go_up])
    fourth = feed_forward([(far, s_far)], [g_far], w_gate, w_up, w_down)
    groups = (near, second, third, fourth)
    part = sum(group[5] for group in groups) / gain
    p_far, p_far_side = fourth[6:]
    part_side, got = pair(part), pair(p_far_side)
    d_w_down = weight_gradient([group[2] for group in groups], [group[1] for group in groups], "d_w_down")
    a, b, c = tie([a, b, c], [part_side, got, d_w_down])
    sums = [a, b, c, p_u2, p_d2, low_u1, low_d1, p_far, got, part, part_side]
    go_up, go_dn, straight = add_step(second_sums, sums, (wide + 16, wide + 16, rows))
    a, b, c = other(go_dn), first(go_up), pair(high1)
    row_parts = tie([group[0] for group in groups], [go_up])
    d_w_gate = weight_gradient(row_parts, [group[3] for group in groups], "d_w_gate")
    a, b, c = tie([a, b, c], [d_w_gate])
    sums = [a, b, c, p_u1, p_d1, own_side, part, part_side]
    go_up, go_dn, go_side, around = add_step(last_sums, sums, (rows + 16, rows + 16, rows, F32))
    straight = opposite(straight, size)
    row_parts = tie([group[0] for group in groups], [go_up, straight])
    d_w_up = weight_gradient(row_parts, [group[4] for group in groups], "d_w_up")
    arrived = tie([other(go_dn), first(go_up), pair(go_side), straight], [d_w_up])

    d_summed, outgoing, five = token_gradient(own, arrived, around, grad_out, normed, scale, gain, heads)
    (around,) = tie([around], [outgoing])
    d_gain = total_gain(five, opposite(around, size))
    d_tokens = add_heads(d_summed, exchange(outgoing))
    return d_tokens[:, None], d_w_gate[None], d_w_up[None], d_w_down[None], d_gain


def solution(mesh):
    placed = (
        P("dp", "token", None),
        P("dp", "token", None),
        P("token", None),
        P("token", None, "dp"),
        P("token", None, "dp"),
        P("token", "dp", None),
    )
    return jax.shard_map(
        shards,
        mesh=mesh,
        in_specs=placed,
        out_specs=(
            P("dp", "token", None),
            P("token", None, "dp"),
            P("token", None, "dp"),
            P("token", "dp", None),
            P("token", None),
        ),
        check_vma=False,
    )
```

```python
import jax
import jax.numpy as jnp
from jax import lax
from jax.experimental import pallas as pl
from jax.experimental.pallas import tpu as pltpu
from jax.sharding import PartitionSpec as P

BF = jnp.bfloat16
F32 = jnp.float32
VMEM = 40 * 1024 * 1024
ROWS_IN = ((0,), (0,))
COLUMNS_OUT = ((1,), (0,))
COLUMNS_IN = ((1,), (1,))
HBM = pl.BlockSpec(memory_space=pl.ANY)


def moves(size):
    ring = size // 2

    def swap(partner):
        pairs = [(z * 2 + x, (partner(z) % ring) * 2 + x) for z in range(ring) for x in range(2)]
        return lambda block: lax.ppermute(block, "dp", pairs)

    first = swap(lambda z: z + 1 if z % 2 == 0 else z - 1)
    other = swap(lambda z: z - 1 if z % 2 == 0 else z + 1)
    return first, other, lambda block: lax.ppermute(block, "dp", [(at, at ^ 1) for at in range(size)])


def tie(values, others):
    return lax.optimization_barrier((tuple(values), tuple(others)))[0]


def opposite(block, size):
    return lax.ppermute(block, "dp", [(at, (at + size // 2) % size) for at in range(size)])


def dot(a, b, dims):
    return lax.dot_general(a, b, (dims, ((), ())), preferred_element_type=F32)


def kernel(body, shapes, args, name, flops=0, specs=None, scratch=()):
    outs = tuple(jax.ShapeDtypeStruct(shape, kind) for shape, kind in shapes)
    moved = sum(a.size * a.dtype.itemsize for a in args) + sum(o.size * o.dtype.itemsize for o in outs)
    whole = pl.BlockSpec(memory_space=pltpu.VMEM)
    return pl.pallas_call(
        body,
        out_shape=outs,
        in_specs=[whole] * len(args) if specs is None else specs,
        out_specs=tuple(whole for _ in outs),
        scratch_shapes=list(scratch),
        compiler_params=pltpu.CompilerParams(vmem_limit_bytes=VMEM),
        cost_estimate=pl.CostEstimate(flops=flops, bytes_accessed=moved, transcendentals=0),
        name=name,
    )(*args)


def put_heads(ref, whole):
    size = ref.shape[2]
    for head in range(ref.shape[0]):
        ref[head] = whole[:, head * size : (head + 1) * size].astype(BF)


def take_heads(ref):
    return jnp.concatenate([ref[head].astype(F32) for head in range(ref.shape[0])], axis=1)


def split_heads(source, heads):
    rows, features = source.shape

    def body(source_ref, out_ref):
        put_heads(out_ref, source_ref[...].astype(F32))

    return kernel(body, [((heads, rows, features // heads), BF)], [source], "split_heads")[0]


def normalize(arrived, tokens, gain):
    rows, features = tokens.shape

    def body(arrived_ref, tokens_ref, gain_ref, hidden_ref, normed_ref, scale_ref):
        summed = tokens_ref[...].astype(F32) + take_heads(arrived_ref)
        scale = lax.rsqrt(jnp.mean(summed * summed, axis=-1, keepdims=True) + 1e-06)
        normed = summed * scale
        hidden_ref[...] = (normed * gain_ref[...]).astype(BF)
        normed_ref[...] = normed
        scale_ref[...] = jnp.broadcast_to(scale, (rows, 128))

    shapes = [((rows, features), BF), ((rows, features), F32), ((rows, 128), F32)]
    return kernel(body, shapes, [arrived, tokens, gain], "normalize", flops=30 * 10**9)


def token_gradient(own, arrived, around, grad_out, normed, scale, gain, heads):
    rows, features = grad_out.shape

    def body(own_ref, a_ref, b_ref, c_ref, d_ref, near_ref, grad_ref, normed_ref, scale_ref, gain_ref, sum_ref, heads_ref, total_ref):
        d_hidden = own_ref[...].astype(F32)
        for ref in (a_ref, b_ref, c_ref, d_ref):
            d_hidden = d_hidden + ref[:rows, :].astype(F32)
        scaled = d_hidden * gain_ref[...]
        normed = normed_ref[...]
        mean = jnp.mean(scaled * normed, axis=-1, keepdims=True)
        d_summed = grad_ref[...].astype(F32) + scale_ref[:, :1] * (scaled - normed * mean)
        sum_ref[...] = d_summed
        put_heads(heads_ref, d_summed)
        total_ref[...] = near_ref[...] + word_sum(a_ref[rows:, :].astype(F32)) + word_sum(b_ref[rows:, :].astype(F32))

    shapes = [((rows, features), F32), ((heads, rows, features // heads), BF), ((1, features), F32)]
    return kernel(body, shapes, [own, *arrived, around, grad_out, normed, scale, gain], "token_gradient")


def total_gain(one, two):
    def body(one_ref, two_ref, out_ref):
        out_ref[...] = one_ref[...] + two_ref[...]

    return kernel(body, [(one.shape, F32)], [one, two], "total_gain", flops=10**9)[0]


def add_heads(d_summed, arrived):
    def body(sum_ref, arrived_ref, out_ref):
        out_ref[...] = (sum_ref[...] + take_heads(arrived_ref)).astype(BF)

    return kernel(body, [(d_summed.shape, BF)], [d_summed, arrived], "add_heads")[0]


def join_two(one, two):
    rows, features = one.shape

    def body(one_ref, two_ref, out_ref, sems):
        copies = [pltpu.make_async_copy(ref, out_ref.at[pl.ds(at * rows, rows)], sems.at[at]) for at, ref in enumerate((one_ref, two_ref))]
        for copy in copies:
            copy.start()
        for copy in copies:
            copy.wait()

    return kernel(body, [((2 * rows, features), BF)], [one, two], "join_two", flops=20 * 10**9, specs=[HBM] * 2, scratch=[pltpu.SemaphoreType.DMA((2,))])[0]


def feed_forward(blocks, grads, w_gate, w_up, w_down):
    rows = blocks[0][0].shape[0]
    flat = [block for two in blocks for block in two]
    count = len(flat) * rows
    features, units = w_gate.shape
    half = rows // 2
    alone, paired = len(blocks) % 2, len(blocks) // 2
    n_in = len(flat) + len(grads) + 3

    def body(*refs):
        row_refs, grad_refs = refs[: len(flat)], refs[len(flat) : n_in - 3]
        wg_ref, wu_ref, wd_ref = refs[n_in - 3 : n_in]
        row_ref, grad_ref, act_ref, dg_ref, du_ref, gain_ref = refs[n_in : n_in + 6]
        part_refs = refs[n_in + 6 :]
        for whole, pieces in ((row_ref, row_refs), (grad_ref, grad_refs)):
            at = 0
            for piece in pieces:
                whole[at : at + piece.shape[0], :] = piece[...]
                at += piece.shape[0]
        row = row_ref[...]
        gate_out = dot(row, wg_ref[...], COLUMNS_OUT)
        up_out = dot(row, wu_ref[...], COLUMNS_OUT)
        d_activation = dot(grad_ref[...], wd_ref[...], COLUMNS_IN)
        sigmoid_gate = jax.nn.sigmoid(gate_out)
        silu_gate = gate_out * sigmoid_gate
        act_ref[...] = (silu_gate * up_out).astype(BF)
        silu_slope = sigmoid_gate * (1.0 + gate_out * (1.0 - sigmoid_gate))
        d_gate_pre = (d_activation * up_out * silu_slope).astype(BF)
        d_up_pre = (d_activation * silu_gate).astype(BF)
        dg_ref[...] = d_gate_pre
        du_ref[...] = d_up_pre
        part = dot(d_gate_pre, wg_ref[...], COLUMNS_IN) + dot(d_up_pre, wu_ref[...], COLUMNS_IN)
        gain_ref[...] = jnp.sum(part * row_ref[...].astype(F32), axis=0, keepdims=True)
        part = part.astype(BF)
        at, out = 0, iter(part_refs)
        for _ in range(alone):
            next(out)[...] = part[at : at + rows]
            next(out)[...] = part[at + rows : at + 2 * rows]
            at += 2 * rows
        for _ in range(paired):
            up, up_side, dn, dn_side = (part[at + i * rows : at + (i + 1) * rows] for i in range(4))
            for whole in (up, dn):
                next(out)[...] = whole
            for piece in (up_side[:half], dn_side[:half]):
                next(out)[...] = piece
            high = next(out)
            high[:half] = up_side[half:]
            high[half:] = dn_side[half:]
            at += 4 * rows

    wide, thin, piece, short = ((count, features), BF), ((count, units), BF), ((rows, features), BF), ((half, features), BF)
    shapes = [wide, wide, thin, thin, thin, ((1, features), F32)] + [piece] * (2 * alone) + [piece, piece, short, short, piece] * paired
    return kernel(body, shapes, [*flat, *grads, w_gate, w_up, w_down], "feed_forward", flops=10 * count * features * units)


def two_words(value):
    high = value.astype(BF).astype(F32)
    at = lax.broadcasted_iota(jnp.int32, (16, value.shape[1]), 0)
    return jnp.where(at == 0, high, jnp.where(at == 1, value - high, 0.0))


def word_sum(rows):
    return jnp.sum(rows, axis=0, keepdims=True)


def add_step(step, args, widths):
    features = args[0].shape[1]
    count = len(args)

    def body(*refs):
        for out, parts in zip(refs[count:], step([ref[...].astype(F32) for ref in refs[:count]])):
            at = 0
            for part in parts:
                out[at : at + part.shape[0], :] = part.astype(out.dtype)
                at += part.shape[0]

    shapes = [((1, features), F32) if width is F32 else ((width, features), BF) for width in widths]
    return kernel(body, shapes, args, "add_step")


def weight_gradient(lefts, rights, name):
    count, shape = len(lefts), (lefts[0].shape[1], rights[0].shape[1])

    def body(*refs):
        total = dot(refs[0][...], refs[count][...], ROWS_IN)
        for at in range(1, count):
            total = total + dot(refs[at][...], refs[count + at][...], ROWS_IN)
        refs[-1][...] = total.astype(BF)

    rows = sum(left.shape[0] for left in lefts)
    return kernel(body, [(shape, BF)], [*lefts, *rights], name, flops=2 * rows * shape[0] * shape[1])[0]


def shards(tokens, grad_out, gain, w_gate, w_up, w_down):
    rows = tokens.shape[0]
    half = rows // 2
    wide = rows + half
    heads, size = lax.axis_size("token"), lax.axis_size("dp")
    first, other, pair = moves(size)
    w_gate, w_up, w_down = w_gate[0], w_up[0], w_down[0]

    def exchange(blocks):
        return lax.all_to_all(blocks, "token", split_axis=0, concat_axis=0, tiled=True)

    tokens, grad_out = tokens[:, 0], grad_out[:, 0]
    g_s0 = pair(grad_out)
    mixed_in = exchange(split_heads(tokens, heads))
    hidden_in, normed, scale = normalize(mixed_in, tokens, gain)
    g0 = join_two(grad_out, g_s0)

    u1, d1, s0 = first(hidden_in), other(hidden_in), pair(hidden_in)
    g_u1, g_d1 = first(g0), other(g0)
    u2, d2, s_u1, s_d1 = first(d1), other(u1), pair(u1), pair(d1)
    g_u2, g_d2 = first(g_d1), other(g_u1)
    u2, d2 = tie([u2, d2], [s0])
    u3, d3 = first(d2), other(u2)
    u2, d2 = tie([u2, d2], [s_u1, s_d1])
    s_u2, s_d2 = pair(u2), pair(d2)
    g_u3, g_d3 = first(g_d2), other(g_u2)
    s_u3, s_d3, far = pair(u3), pair(d3), other(u3)
    g_far = first(g_d3)
    near = feed_forward([(hidden_in, s0), (u1, s_u1), (d1, s_d1)], [g0, g_u1, g_d1], w_gate, w_up, w_down)
    second = feed_forward([(u2, s_u2), (d2, s_d2)], [g_u2, g_d2], w_gate, w_up, w_down)
    s_u3, s_d3 = tie([s_u3, s_d3], [near[6], second[6], far])
    third = feed_forward([(u3, s_u3), (d3, s_d3)], [g_u3, g_d3], w_gate, w_up, w_down)

    own, own_side, p_u1, p_d1, low_u1, low_d1, high1 = near[6:]
    p_u2, p_d2, low_u2, low_d2, high2 = second[6:]
    p_u3, p_d3, low_u3, low_d3, high3 = third[6:]

    def first_sums(v):
        a, b, c, up, dn, up_low, dn_low = v
        return [(up[:half], up[half:] + c[:half], up_low + a), (dn[:half], dn[half:] + c[half:], dn_low + b)]

    def second_sums(v):
        a, b, c, up, dn, up_low, dn_low, p_far, got, one, two = v
        spare = two_words(one + two)
        go_up = (up[:half] + a[:half], up[half:] + a[half:rows] + c[:half], up_low + a[rows:], spare)
        go_dn = (dn[:half] + b[:half], dn[half:] + b[half:rows] + c[half:], dn_low + b[rows:], spare)
        return [go_up, go_dn, (p_far + got,)]

    def last_sums(v):
        a, b, c, up, dn, side, one, two = v
        go_up = (up[:half] + a[:half], up[half:] + a[half:rows] + c[:half], a[wide:])
        go_dn = (dn[:half] + b[:half], dn[half:] + b[half:rows] + c[half:], b[wide:])
        around = one + two + word_sum(a[wide:]) + word_sum(b[wide:])
        return [go_up, go_dn, (side[:half] + a[rows:wide] + b[rows:wide], side[half:]), (around,)]

    a, b, c, s_far = other(low_d3), first(low_u3), pair(high3), pair(far)
    go_up, go_dn = add_step(first_sums, [a, b, c, p_u3, p_d3, low_u2, low_d2], (wide, wide))
    a, b, c = other(go_dn), first(go_up), pair(high2)
    (s_far,) = tie([s_far], [go_up])
    fourth = feed_forward([(far, s_far)], [g_far], w_gate, w_up, w_down)
    groups = (near, second, third, fourth)
    part = sum(group[5] for group in groups) / gain
    p_far, p_far_side = fourth[6:]
    part_side, got = pair(part), pair(p_far_side)
    d_w_down = weight_gradient([group[2] for group in groups], [group[1] for group in groups], "d_w_down")
    a, b, c = tie([a, b, c], [part_side, got, d_w_down])
    sums = [a, b, c, p_u2, p_d2, low_u1, low_d1, p_far, got, part, part_side]
    go_up, go_dn, straight = add_step(second_sums, sums, (wide + 16, wide + 16, rows))
    a, b, c = other(go_dn), first(go_up), pair(high1)
    row_parts = tie([group[0] for group in groups], [go_up])
    d_w_gate = weight_gradient(row_parts, [group[3] for group in groups], "d_w_gate")
    a, b, c = tie([a, b, c], [d_w_gate])
    sums = [a, b, c, p_u1, p_d1, own_side, part, part_side]
    go_up, go_dn, go_side, around = add_step(last_sums, sums, (rows + 16, rows + 16, rows, F32))
    straight = opposite(straight, size)
    row_parts = tie([group[0] for group in groups], [go_up, straight])
    d_w_up = weight_gradient(row_parts, [group[4] for group in groups], "d_w_up")
    arrived = tie([other(go_dn), first(go_up), pair(go_side), straight], [d_w_up])

    d_summed, outgoing, five = token_gradient(own, arrived, around, grad_out, normed, scale, gain, heads)
    (around,) = tie([around], [outgoing])
    d_gain = total_gain(five, opposite(around, size))
    d_tokens = add_heads(d_summed, exchange(outgoing))
    return d_tokens[:, None], d_w_gate[None], d_w_up[None], d_w_down[None], d_gain


def solution(mesh):
    placed = (
        P("dp", "token", None),
        P("dp", "token", None),
        P("token", None),
        P("token", None, "dp"),
        P("token", None, "dp"),
        P("token", "dp", None),
    )
    return jax.shard_map(
        shards,
        mesh=mesh,
        in_specs=placed,
        out_specs=(
            P("dp", "token", None),
            P("token", None, "dp"),
            P("token", None, "dp"),
            P("token", "dp", None),
            P("token", None),
        ),
        check_vma=False,
    )
```

```python
import jax
import jax.numpy as jnp
from jax import lax
from jax.experimental import pallas as pl
from jax.experimental.pallas import tpu as pltpu
from jax.sharding import PartitionSpec as P

BF = jnp.bfloat16
F32 = jnp.float32
VMEM = 40 * 1024 * 1024
ROWS_IN = ((0,), (0,))
COLUMNS_OUT = ((1,), (0,))
COLUMNS_IN = ((1,), (1,))
HBM = pl.BlockSpec(memory_space=pl.ANY)


def moves(size):
    ring = size // 2

    def swap(partner):
        pairs = [(z * 2 + x, (partner(z) % ring) * 2 + x) for z in range(ring) for x in range(2)]
        return lambda block: lax.ppermute(block, "dp", pairs)

    first = swap(lambda z: z + 1 if z % 2 == 0 else z - 1)
    other = swap(lambda z: z - 1 if z % 2 == 0 else z + 1)
    return first, other, lambda block: lax.ppermute(block, "dp", [(at, at ^ 1) for at in range(size)])


def tie(values, others):
    return lax.optimization_barrier((tuple(values), tuple(others)))[0]


def opposite(block, size):
    return lax.ppermute(block, "dp", [(at, (at + size // 2) % size) for at in range(size)])


def dot(a, b, dims):
    return lax.dot_general(a, b, (dims, ((), ())), preferred_element_type=F32)


def kernel(body, shapes, args, name, flops=0, specs=None, scratch=()):
    outs = tuple(jax.ShapeDtypeStruct(shape, kind) for shape, kind in shapes)
    moved = sum(a.size * a.dtype.itemsize for a in args) + sum(o.size * o.dtype.itemsize for o in outs)
    whole = pl.BlockSpec(memory_space=pltpu.VMEM)
    return pl.pallas_call(
        body,
        out_shape=outs,
        in_specs=[whole] * len(args) if specs is None else specs,
        out_specs=tuple(whole for _ in outs),
        scratch_shapes=list(scratch),
        compiler_params=pltpu.CompilerParams(vmem_limit_bytes=VMEM),
        cost_estimate=pl.CostEstimate(flops=flops, bytes_accessed=moved, transcendentals=0),
        name=name,
    )(*args)


def put_heads(ref, whole):
    tall, lanes = ref.shape[1:]
    size = tall * lanes // whole.shape[0]
    spare = lanes - size
    short = whole.shape[0] - tall
    for head in range(ref.shape[0]):
        block = whole[:, head * size : (head + 1) * size]
        rest = [block[tall:, at * spare : (at + 1) * spare] for at in range(tall // short)]
        ref[head] = jnp.concatenate([block[:tall], jnp.concatenate(rest, axis=0)], axis=1).astype(BF)


def take_heads(ref, rows):
    tall, lanes = ref.shape[1:]
    size = tall * lanes // rows
    short = rows - tall
    blocks = []
    for head in range(ref.shape[0]):
        block = ref[head].astype(F32)
        rest = [block[at * short : (at + 1) * short, size:] for at in range(tall // short)]
        blocks.append(jnp.concatenate([block[:, :size], jnp.concatenate(rest, axis=1)], axis=0))
    return jnp.concatenate(blocks, axis=1)


def split_heads(source, heads):
    rows, features = source.shape

    def body(source_ref, out_ref):
        put_heads(out_ref, source_ref[...].astype(F32))

    return kernel(body, [((heads, rows * features // heads // 128, 128), BF)], [source], "split_heads")[0]


def normalize(arrived, tokens, gain):
    rows, features = tokens.shape

    def body(arrived_ref, tokens_ref, gain_ref, hidden_ref, normed_ref, scale_ref):
        summed = tokens_ref[...].astype(F32) + take_heads(arrived_ref, rows)
        scale = lax.rsqrt(jnp.mean(summed * summed, axis=-1, keepdims=True) + 1e-06)
        normed = summed * scale
        hidden_ref[...] = (normed * gain_ref[...]).astype(BF)
        normed_ref[...] = normed
        scale_ref[...] = jnp.broadcast_to(scale, (rows, 128))

    shapes = [((rows, features), BF), ((rows, features), F32), ((rows, 128), F32)]
    return kernel(body, shapes, [arrived, tokens, gain], "normalize", flops=30 * 10**9)


def token_gradient(own, arrived, around, grad_out, normed, scale, gain, heads):
    rows, features = grad_out.shape

    def body(own_ref, a_ref, b_ref, c_ref, d_ref, near_ref, grad_ref, normed_ref, scale_ref, gain_ref, sum_ref, heads_ref, total_ref):
        d_hidden = own_ref[...].astype(F32)
        for ref in (a_ref, b_ref, c_ref, d_ref):
            d_hidden = d_hidden + ref[:rows, :].astype(F32)
        scaled = d_hidden * gain_ref[...]
        normed = normed_ref[...]
        mean = jnp.mean(scaled * normed, axis=-1, keepdims=True)
        d_summed = grad_ref[...].astype(F32) + scale_ref[:, :1] * (scaled - normed * mean)
        sum_ref[...] = d_summed
        put_heads(heads_ref, d_summed)
        total_ref[...] = near_ref[...] + word_sum(a_ref[rows:, :].astype(F32)) + word_sum(b_ref[rows:, :].astype(F32))

    shapes = [((rows, features), F32), ((heads, rows * features // heads // 128, 128), BF), ((1, features), F32)]
    return kernel(body, shapes, [own, *arrived, around, grad_out, normed, scale, gain], "token_gradient")


def total_gain(one, two):
    def body(one_ref, two_ref, out_ref):
        out_ref[...] = one_ref[...] + two_ref[...]

    return kernel(body, [(one.shape, F32)], [one, two], "total_gain", flops=10**9)[0]


def add_heads(d_summed, arrived):
    def body(sum_ref, arrived_ref, out_ref):
        out_ref[...] = (sum_ref[...] + take_heads(arrived_ref, sum_ref.shape[0])).astype(BF)

    return kernel(body, [(d_summed.shape, BF)], [d_summed, arrived], "add_heads")[0]


def join_two(one, two):
    rows, features = one.shape

    def body(one_ref, two_ref, out_ref, sems):
        copies = [pltpu.make_async_copy(ref, out_ref.at[pl.ds(at * rows, rows)], sems.at[at]) for at, ref in enumerate((one_ref, two_ref))]
        for copy in copies:
            copy.start()
        for copy in copies:
            copy.wait()

    return kernel(body, [((2 * rows, features), BF)], [one, two], "join_two", flops=20 * 10**9, specs=[HBM] * 2, scratch=[pltpu.SemaphoreType.DMA((2,))])[0]


def feed_forward(blocks, grads, w_gate, w_up, w_down):
    rows = blocks[0][0].shape[0]
    flat = [block for two in blocks for block in two]
    count = len(flat) * rows
    features, units = w_gate.shape
    half = rows // 2
    alone, paired = len(blocks) % 2, len(blocks) // 2
    n_in = len(flat) + len(grads) + 3

    def body(*refs):
        row_refs, grad_refs = refs[: len(flat)], refs[len(flat) : n_in - 3]
        wg_ref, wu_ref, wd_ref = refs[n_in - 3 : n_in]
        row_ref, grad_ref, act_ref, dg_ref, du_ref, gain_ref = refs[n_in : n_in + 6]
        part_refs = refs[n_in + 6 :]
        for whole, pieces in ((row_ref, row_refs), (grad_ref, grad_refs)):
            at = 0
            for piece in pieces:
                whole[at : at + piece.shape[0], :] = piece[...]
                at += piece.shape[0]
        row = row_ref[...]
        gate_out = dot(row, wg_ref[...], COLUMNS_OUT)
        up_out = dot(row, wu_ref[...], COLUMNS_OUT)
        d_activation = dot(grad_ref[...], wd_ref[...], COLUMNS_IN)
        sigmoid_gate = jax.nn.sigmoid(gate_out)
        silu_gate = gate_out * sigmoid_gate
        act_ref[...] = (silu_gate * up_out).astype(BF)
        silu_slope = sigmoid_gate * (1.0 + gate_out * (1.0 - sigmoid_gate))
        d_gate_pre = (d_activation * up_out * silu_slope).astype(BF)
        d_up_pre = (d_activation * silu_gate).astype(BF)
        dg_ref[...] = d_gate_pre
        du_ref[...] = d_up_pre
        part = dot(d_gate_pre, wg_ref[...], COLUMNS_IN) + dot(d_up_pre, wu_ref[...], COLUMNS_IN)
        gain_ref[...] = jnp.sum(part * row_ref[...].astype(F32), axis=0, keepdims=True)
        part = part.astype(BF)
        at, out = 0, iter(part_refs)
        for _ in range(alone):
            next(out)[...] = part[at : at + rows]
            next(out)[...] = part[at + rows : at + 2 * rows]
            at += 2 * rows
        for _ in range(paired):
            up, up_side, dn, dn_side = (part[at + i * rows : at + (i + 1) * rows] for i in range(4))
            for whole in (up, dn):
                next(out)[...] = whole
            for piece in (up_side[:half], dn_side[:half]):
                next(out)[...] = piece
            high = next(out)
            high[:half] = up_side[half:]
            high[half:] = dn_side[half:]
            at += 4 * rows

    wide, thin, piece, short = ((count, features), BF), ((count, units), BF), ((rows, features), BF), ((half, features), BF)
    shapes = [wide, wide, thin, thin, thin, ((1, features), F32)] + [piece] * (2 * alone) + [piece, piece, short, short, piece] * paired
    return kernel(body, shapes, [*flat, *grads, w_gate, w_up, w_down], "feed_forward", flops=10 * count * features * units)


def two_words(value):
    high = value.astype(BF).astype(F32)
    at = lax.broadcasted_iota(jnp.int32, (16, value.shape[1]), 0)
    return jnp.where(at == 0, high, jnp.where(at == 1, value - high, 0.0))


def word_sum(rows):
    return jnp.sum(rows, axis=0, keepdims=True)


def add_step(step, args, widths):
    features = args[0].shape[1]
    count = len(args)

    def body(*refs):
        for out, parts in zip(refs[count:], step([ref[...].astype(F32) for ref in refs[:count]])):
            at = 0
            for part in parts:
                out[at : at + part.shape[0], :] = part.astype(out.dtype)
                at += part.shape[0]

    shapes = [((1, features), F32) if width is F32 else ((width, features), BF) for width in widths]
    return kernel(body, shapes, args, "add_step")


def weight_gradient(lefts, rights, name):
    count, shape = len(lefts), (lefts[0].shape[1], rights[0].shape[1])

    def body(*refs):
        total = dot(refs[0][...], refs[count][...], ROWS_IN)
        for at in range(1, count):
            total = total + dot(refs[at][...], refs[count + at][...], ROWS_IN)
        refs[-1][...] = total.astype(BF)

    rows = sum(left.shape[0] for left in lefts)
    return kernel(body, [(shape, BF)], [*lefts, *rights], name, flops=2 * rows * shape[0] * shape[1])[0]


def shards(tokens, grad_out, gain, w_gate, w_up, w_down):
    rows = tokens.shape[0]
    half = rows // 2
    wide = rows + half
    heads, size = lax.axis_size("token"), lax.axis_size("dp")
    first, other, pair = moves(size)
    w_gate, w_up, w_down = w_gate[0], w_up[0], w_down[0]

    def exchange(blocks):
        return lax.all_to_all(blocks, "token", split_axis=0, concat_axis=0, tiled=True)

    tokens, grad_out = tokens[:, 0], grad_out[:, 0]
    g_s0 = pair(grad_out)
    mixed_in = exchange(split_heads(tokens, heads))
    hidden_in, normed, scale = normalize(mixed_in, tokens, gain)
    g0 = join_two(grad_out, g_s0)

    u1, d1, s0 = first(hidden_in), other(hidden_in), pair(hidden_in)
    g_u1, g_d1 = first(g0), other(g0)
    u2, d2, s_u1, s_d1 = first(d1), other(u1), pair(u1), pair(d1)
    g_u2, g_d2 = first(g_d1), other(g_u1)
    u2, d2 = tie([u2, d2], [s0])
    u3, d3 = first(d2), other(u2)
    u2, d2 = tie([u2, d2], [s_u1, s_d1])
    s_u2, s_d2 = pair(u2), pair(d2)
    g_u3, g_d3 = first(g_d2), other(g_u2)
    s_u3, s_d3, far = pair(u3), pair(d3), other(u3)
    g_far = first(g_d3)
    near = feed_forward([(hidden_in, s0), (u1, s_u1), (d1, s_d1)], [g0, g_u1, g_d1], w_gate, w_up, w_down)
    second = feed_forward([(u2, s_u2), (d2, s_d2)], [g_u2, g_d2], w_gate, w_up, w_down)
    s_u3, s_d3 = tie([s_u3, s_d3], [near[6], second[6], far])
    third = feed_forward([(u3, s_u3), (d3, s_d3)], [g_u3, g_d3], w_gate, w_up, w_down)

    own, own_side, p_u1, p_d1, low_u1, low_d1, high1 = near[6:]
    p_u2, p_d2, low_u2, low_d2, high2 = second[6:]
    p_u3, p_d3, low_u3, low_d3, high3 = third[6:]

    def first_sums(v):
        a, b, c, up, dn, up_low, dn_low = v
        return [(up[:half], up[half:] + c[:half], up_low + a), (dn[:half], dn[half:] + c[half:], dn_low + b)]

    def second_sums(v):
        a, b, c, up, dn, up_low, dn_low, p_far, got, one, two = v
        spare = two_words(one + two)
        go_up = (up[:half] + a[:half], up[half:] + a[half:rows] + c[:half], up_low + a[rows:], spare)
        go_dn = (dn[:half] + b[:half], dn[half:] + b[half:rows] + c[half:], dn_low + b[rows:], spare)
        return [go_up, go_dn, (p_far + got,)]

    def last_sums(v):
        a, b, c, up, dn, side, one, two = v
        go_up = (up[:half] + a[:half], up[half:] + a[half:rows] + c[:half], a[wide:])
        go_dn = (dn[:half] + b[:half], dn[half:] + b[half:rows] + c[half:], b[wide:])
        around = one + two + word_sum(a[wide:]) + word_sum(b[wide:])
        return [go_up, go_dn, (side[:half] + a[rows:wide] + b[rows:wide], side[half:]), (around,)]

    a, b, c, s_far = other(low_d3), first(low_u3), pair(high3), pair(far)
    go_up, go_dn = add_step(first_sums, [a, b, c, p_u3, p_d3, low_u2, low_d2], (wide, wide))
    a, b, c = other(go_dn), first(go_up), pair(high2)
    (s_far,) = tie([s_far], [go_up])
    fourth = feed_forward([(far, s_far)], [g_far], w_gate, w_up, w_down)
    groups = (near, second, third, fourth)
    part = sum(group[5] for group in groups) / gain
    p_far, p_far_side = fourth[6:]
    part_side, got = pair(part), pair(p_far_side)
    d_w_down = weight_gradient([group[2] for group in groups], [group[1] for group in groups], "d_w_down")
    a, b, c = tie([a, b, c], [part_side, got, d_w_down])
    sums = [a, b, c, p_u2, p_d2, low_u1, low_d1, p_far, got, part, part_side]
    go_up, go_dn, straight = add_step(second_sums, sums, (wide + 16, wide + 16, rows))
    a, b, c = other(go_dn), first(go_up), pair(high1)
    row_parts = tie([group[0] for group in groups], [go_up])
    d_w_gate = weight_gradient(row_parts, [group[3] for group in groups], "d_w_gate")
    a, b, c = tie([a, b, c], [d_w_gate])
    sums = [a, b, c, p_u1, p_d1, own_side, part, part_side]
    go_up, go_dn, go_side, around = add_step(last_sums, sums, (rows + 16, rows + 16, rows, F32))
    straight = opposite(straight, size)
    row_parts = tie([group[0] for group in groups], [go_up, straight])
    d_w_up = weight_gradient(row_parts, [group[4] for group in groups], "d_w_up")
    arrived = tie([other(go_dn), first(go_up), pair(go_side), straight], [d_w_up])

    d_summed, outgoing, five = token_gradient(own, arrived, around, grad_out, normed, scale, gain, heads)
    (around,) = tie([around], [outgoing])
    d_gain = total_gain(five, opposite(around, size))
    d_tokens = add_heads(d_summed, exchange(outgoing))
    return d_tokens[:, None], d_w_gate[None], d_w_up[None], d_w_down[None], d_gain


def solution(mesh):
    placed = (
        P("dp", "token", None),
        P("dp", "token", None),
        P("token", None),
        P("token", None, "dp"),
        P("token", None, "dp"),
        P("token", "dp", None),
    )
    return jax.shard_map(
        shards,
        mesh=mesh,
        in_specs=placed,
        out_specs=(
            P("dp", "token", None),
            P("token", None, "dp"),
            P("token", None, "dp"),
            P("token", "dp", None),
            P("token", None),
        ),
        check_vma=False,
    )
```
